256 devices in a mesh: rows: 64 (over x, z, core), pairs: 4 (over y).
Axes of the slice: x: 4, y: 4, z: 8, core: 2. Of those that a mesh axis runs over, the one named last changes fastest.
Arguments:
- embeddings: float32 [32768, 512], P('rows'), may hold values from -5.6 to 5.6
- start_basis: float32 [32768, 64], P('rows'), may hold values from -6 to 6
- pair_mask: int32 [64, 5], P('rows'), may hold values from 0 to 1, as said below
Outputs:
- final_basis: float32 [32768, 64], P('rows')
- projected: float32 [64, 64], replicated
The draws below stay inside these ranges and needn't reach their ends.
Inputs may be any that keep to these rules, and one draw needn't show every extreme that they name: `pair_mask`: offset 0 is listed for every row block, offsets past the last block never; each row block lists 1 to 4 pairs, the first row block exactly 4.
All inputs are finite; a program needn't handle non-finite values.
Results may differ from the reference program's by a relative error of at most 0.017.
Values may be sent and summed in bfloat16 or wider, within the bound.
No kernel may reach another device: no remote copies, remote signals or barrier semaphores. Data moves between devices by JAX's collectives and lax.ppermute only.
A program may use at most 64 MiB of HBM per device.

```python
import math
import jax
import jax.numpy as jnp
from jax import lax

WIDTH = 512
BASIS = 64
BLOCK = 512
REACH = 5
MOST = 4
ITERS = 2
NBLK = 64
DOCS = 32768


latent_dims = 8


def draw_pair_mask(key, part):
    key = jax.random.fold_in(key, 7)
    count_key, score_key = jax.random.split(key)
    extra_count = jax.random.randint(count_key, (NBLK,), 0, MOST, dtype=jnp.int32)
    extra_count = extra_count.at[0].set(MOST - 1)
    offsets = jnp.arange(1, REACH, dtype=jnp.int32)
    draw_scores = jax.random.randint(score_key, (NBLK, REACH - 1), 0, 4096, dtype=jnp.int32)
    scores = (draw_scores - 600 * offsets[None, :]) * REACH + (REACH - offsets[None, :])
    standing = jnp.sum((scores[:, None, :] > scores[:, :, None]).astype(jnp.int32), axis=2)
    chosen = standing < extra_count[:, None]
    inside = jnp.arange(NBLK, dtype=jnp.int32)[:, None] + offsets[None, :] < NBLK
    listed = (chosen & inside).astype(jnp.int32)
    return jnp.concatenate([jnp.ones((NBLK, 1), jnp.int32), listed], axis=1)


def draw_embeddings(key, part):
    key = jax.random.fold_in(key, 11)
    latent_key, noise_key = jax.random.split(key)
    copies = WIDTH // latent_dims
    latent = jnp.clip(jax.random.normal(latent_key, (DOCS, latent_dims), jnp.float32), -4.0, 4.0)
    noise = jnp.clip(jax.random.normal(noise_key, (DOCS, WIDTH), jnp.float32), -4.0, 4.0)
    spread = jnp.tile(latent, (1, copies))
    return 0.8 * spread + 0.6 * noise


def level_of(own_key, extent, pieces, least, top_value):
    gain = 1.0
    for dim, parts in pieces:
        draws = jax.random.uniform(jax.random.fold_in(jax.random.fold_in(own_key, 6), dim), (parts,), jnp.float32, least / len(pieces), top_value / len(pieces))
        gain = gain * jnp.repeat(jnp.exp(draws), extent[dim] // parts).reshape((-1,) + (1,) * (len(extent) - 1 - dim))
    return gain


def bell_draw(stream_key, shape, scale, limit, pieces=(), kind=jnp.bfloat16):
    result = jax.random.normal(stream_key, shape, jnp.float32) * scale
    if len(pieces) > 0:
        result = level_of(stream_key, shape, pieces, -0.22, 0.18) * result
    return jnp.clip(result, min=-limit, max=limit).astype(kind)


def setup_inputs(seed: int = 0) -> dict:
    seeds = jax.random.split(jax.random.key(seed), 4)
    embeddings = draw_embeddings(jax.random.fold_in(seeds[3], 71), 0)
    start_basis = bell_draw(seeds[1], (DOCS, BASIS), 1.0, 6.0, ((0, 64),), jnp.float32)
    pair_mask = draw_pair_mask(jax.random.fold_in(seeds[3], 71), 0)
    return {"embeddings": embeddings, "start_basis": start_basis, "pair_mask": pair_mask}


def affinity_tile(left, left_sq, right, right_sq):
    inner = jnp.dot(left.astype(jnp.float32), right.T.astype(jnp.float32), preferred_element_type=jnp.float32)
    distance = left_sq[:, None] + right_sq[None, :] - 2.0 * inner
    return jnp.exp(distance * (-math.log(BLOCK / 4) / (2 * WIDTH))).astype(jnp.bfloat16)

def apply_pairs(rounded, sq_norms, scaled, pair_mask):
    columns = scaled.shape[1]
    blocks = rounded.reshape(NBLK, BLOCK, WIDTH)
    norm_blocks = sq_norms.reshape(NBLK, BLOCK)
    vec_blocks = scaled.reshape(NBLK, BLOCK, columns)
    pad_blocks = jnp.concatenate([blocks, jnp.zeros((REACH, BLOCK, WIDTH), blocks.dtype)])
    pad_norms = jnp.concatenate([norm_blocks, jnp.zeros((REACH, BLOCK), norm_blocks.dtype)])
    pad_vecs = jnp.concatenate([vec_blocks, jnp.zeros((REACH, BLOCK, columns), vec_blocks.dtype)])

    def per_block(index):
        left = lax.dynamic_index_in_dim(blocks, index, 0, False)
        left_sq = lax.dynamic_index_in_dim(norm_blocks, index, 0, False)
        left_vec = lax.dynamic_index_in_dim(vec_blocks, index, 0, False)
        own_term = jnp.zeros((BLOCK, columns), jnp.float32)
        sends = []
        for offset in range(REACH):
            right = lax.dynamic_index_in_dim(pad_blocks, index + offset, 0, False)
            right_sq = lax.dynamic_index_in_dim(pad_norms, index + offset, 0, False)
            right_vec = lax.dynamic_index_in_dim(pad_vecs, index + offset, 0, False)

            def live(right=right, right_sq=right_sq, right_vec=right_vec, offset=offset):
                weights = affinity_tile(left, left_sq, right, right_sq)
                row_term = jnp.dot(weights.astype(jnp.float32), right_vec.astype(jnp.float32), preferred_element_type=jnp.float32)
                if offset > 0:
                    col_term = jnp.dot(weights.T.astype(jnp.float32), left_vec.astype(jnp.float32), preferred_element_type=jnp.float32)
                else:
                    col_term = jnp.zeros((BLOCK, columns), jnp.float32)
                return (row_term, col_term)

            def dead():
                empty = jnp.zeros((BLOCK, columns), jnp.float32)
                return (empty, empty)
            row_term, col_term = lax.cond(pair_mask[index, offset] == 1, live, dead)
            own_term = own_term + row_term
            if offset > 0:
                sends.append(col_term)
        return (own_term, jnp.stack(sends))
    own_terms, sent = lax.map(per_block, jnp.arange(NBLK, dtype=jnp.int32))
    for offset in range(1, REACH):
        moved = jnp.concatenate([jnp.zeros((offset, BLOCK, columns), jnp.float32), sent[:NBLK - offset, offset - 1]])
        own_terms = own_terms + moved
    return own_terms.reshape(DOCS, columns)

def reference(embeddings, start_basis, pair_mask):
    rounded = embeddings.astype(jnp.bfloat16)
    sq_norms = lax.optimization_barrier(jnp.sum(jnp.square(rounded.astype(jnp.float32)), axis=1))
    ones_column = jnp.ones((DOCS, 1), jnp.bfloat16)
    degree = apply_pairs(rounded, sq_norms, ones_column, pair_mask)
    inv_root = lax.rsqrt(degree)
    current = start_basis
    projected = jnp.zeros((BASIS, BASIS), jnp.float32)
    for step in range(ITERS):
        scaled = (current * inv_root).astype(jnp.bfloat16)
        image = inv_root * apply_pairs(rounded, sq_norms, scaled, pair_mask)
        gram_matrix = jnp.dot(image.T.astype(jnp.float32), image.astype(jnp.float32), precision=lax.Precision.HIGHEST, preferred_element_type=jnp.float32) / DOCS
        projected = jnp.dot(current.T.astype(jnp.float32), image.astype(jnp.float32), precision=lax.Precision.HIGHEST, preferred_element_type=jnp.float32) / DOCS
        factor = jnp.linalg.cholesky(gram_matrix)
        current = jax.scipy.linalg.solve_triangular(factor, image.T, lower=True).T
    return (current, projected)
```

```python
import math

import jax
import jax.numpy as jnp
from jax import lax
from jax.sharding import Mesh
from jax.sharding import PartitionSpec as P

WIDTH = 512
BLOCK = 512
CHIPS = 32
CORES = 2
PAIRS = 4
REACHES = ((1, -2), (-1, 2))
ALL_AXES = ("chip", "core", "pairs")


def route(step):
    moves = []
    for chip in range(CHIPS):
        for core in range(CORES):
            for pair in range(PAIRS):
                to_chip, to_core, to_pair = step(chip, core, pair)
                source = (chip * CORES + core) * PAIRS + pair
                target = ((to_chip % CHIPS) * CORES + to_core) * PAIRS + to_pair
                moves.append((source, target))
    return moves


def swap_core(array):
    return lax.ppermute(array, "core", [(0, 1), (1, 0)])


def swap_pair(array):
    return lax.ppermute(array, "pairs", [(i, i ^ 1) for i in range(PAIRS)])


def fetch(array, which):
    moves = route(lambda chip, core, pair: (chip - REACHES[pair % 2][which], core, pair))
    return lax.ppermute(array, ALL_AXES, moves)


def deliver(array, which):
    moves = route(lambda chip, core, pair: (chip + REACHES[pair % 2][which], core, pair))
    return lax.ppermute(array, ALL_AXES, moves)


def listed(reach, own_mask, other_mask, core, row_core):
    offset = 2 * reach + core - row_core
    ahead = jnp.sum(jnp.where(jnp.arange(5) == offset, own_mask, 0.0))
    behind = jnp.sum(jnp.where(jnp.arange(5) == -offset, other_mask, 0.0))
    return jnp.where(offset >= 0, ahead, behind)


def on_device(embeddings, start_basis, pair_mask):
    scale_coef = -math.log(BLOCK / 4) / (2 * WIDTH)
    core = lax.axis_index("core")
    pair = lax.axis_index("pairs")
    parity = pair % 2
    docs_total = BLOCK * CHIPS * CORES

    rounded = embeddings.astype(jnp.bfloat16)
    mask_rows = jnp.pad(pair_mask.astype(jnp.bfloat16), ((0, 15), (0, WIDTH - 5)))
    packed = jnp.concatenate([rounded, mask_rows])
    near = fetch(packed, 0)
    far = fetch(packed, 1)
    mate = swap_core(packed)
    mate_basis = swap_core(start_basis)

    half = BLOCK // 2
    own_half = lax.dynamic_slice_in_dim(rounded, parity * half, half, 0)
    rows = jnp.concatenate([rounded, mate[:BLOCK]])
    cols = jnp.concatenate([near[:BLOCK], far[:BLOCK], own_half])

    def mask_of(array):
        return array[BLOCK, :5].astype(jnp.float32)

    own_mask = pair_mask[0].astype(jnp.float32)
    mate_mask = mask_of(mate)
    flags = []
    for which, source in ((0, near), (1, far), (2, packed)):
        reach = 0 if which == 2 else jnp.where(parity == 0, REACHES[0][which], REACHES[1][which])
        flags.append(
            [
                listed(reach, own_mask, mask_of(source), core, core),
                listed(reach, mate_mask, mask_of(source), core, 1 - core),
            ]
        )
    flag_rows = [jnp.repeat(jnp.stack(f), BLOCK)[None, :] for f in flags]

    def norms(array):
        return jnp.sum(jnp.square(array.astype(jnp.float32)), axis=1)

    rows_sq = norms(rows)
    cols_sq = norms(cols)
    inner = lax.dot_general(
        cols, rows, (((1,), (1,)), ((), ())), preferred_element_type=jnp.float32
    )
    weights = jnp.exp((cols_sq[:, None] + rows_sq[None, :] - 2.0 * inner) * scale_coef)
    flag = jnp.concatenate(
        [
            jnp.broadcast_to(flag_rows[0], (BLOCK, 2 * BLOCK)),
            jnp.broadcast_to(flag_rows[1], (BLOCK, 2 * BLOCK)),
            jnp.broadcast_to(flag_rows[2], (half, 2 * BLOCK)),
        ]
    )
    weights = jnp.where(flag > 0, weights, 0.0).astype(jnp.bfloat16)
    partial_degree = jnp.sum(weights, axis=0, dtype=jnp.float32)
    swapped = swap_core(partial_degree)
    partial_degree = partial_degree + jnp.concatenate([swapped[BLOCK:], swapped[:BLOCK]])
    degree = partial_degree + swap_pair(partial_degree)
    inv_root = lax.rsqrt(degree)[:, None]
    own_root = inv_root[:BLOCK]

    def apply(vectors):
        terms = jnp.dot(weights, vectors, preferred_element_type=jnp.float32)
        if terms.shape[1] == 128:
            terms = terms[:, :64] + terms[:, 64:]
        got = deliver(terms[:BLOCK], 0) + deliver(terms[BLOCK : 2 * BLOCK], 1)
        own = terms[2 * BLOCK :]
        blank = jnp.zeros_like(own)
        own = jnp.where(parity == 0, jnp.concatenate([own, blank]), jnp.concatenate([blank, own]))
        got = got + own
        return got + swap_pair(got)

    scaled = (jnp.concatenate([start_basis, mate_basis]) * inv_root).astype(jnp.bfloat16)
    first = own_root * apply(scaled)
    scaled = own_root * first
    scaled = jnp.concatenate([scaled, swap_core(scaled)])
    high = scaled.astype(jnp.bfloat16)
    low = (scaled - high.astype(jnp.float32)).astype(jnp.bfloat16)
    second = own_root * apply(jnp.concatenate([high, low], axis=1))

    def inner_product(left, right):
        return lax.dot_general(
            left,
            right,
            (((0,), (0,)), ((), ())),
            precision=lax.Precision.HIGHEST,
            preferred_element_type=jnp.float32,
        )

    cross = inner_product(first, second)
    products = jnp.concatenate(
        [
            jnp.concatenate([inner_product(first, first), inner_product(second, second)], axis=1),
            jnp.concatenate([cross[:32], cross[32:]], axis=1),
        ]
    )
    share = 96 // (CORES * PAIRS)
    mine = lax.dynamic_slice_in_dim(products, (core * PAIRS + pair) * share, share, 0)
    theirs = lax.dynamic_slice_in_dim(products, ((1 - core) * PAIRS + pair) * share, share, 0)
    mine = mine + swap_core(theirs)
    gathered = lax.all_to_all(jnp.tile(mine, (CHIPS, 1)), "chip", 0, 0, tiled=True)
    mine = jnp.sum(gathered.reshape(CHIPS, share, 128), axis=0)
    products = lax.all_to_all(
        jnp.tile(mine, (CORES * PAIRS, 1)), ("core", "pairs"), 0, 0, tiled=True
    )
    products = products / docs_total
    gram_first = products[:64, :64]
    gram_second = products[:64, 64:]
    cross = jnp.concatenate([products[64:, :64], products[64:, 64:]])

    eye = jnp.eye(64, dtype=jnp.float32)
    factors = jnp.linalg.cholesky(jnp.stack([gram_first, gram_second]))
    inverses = jax.scipy.linalg.solve_triangular(factors, jnp.stack([eye, eye]), lower=True)
    exact = lax.Precision.HIGHEST
    basis = jnp.dot(second, inverses[1].T, precision=exact)
    projected = jnp.dot(jnp.dot(inverses[0], cross, precision=exact), inverses[0].T, precision=exact)
    return basis, projected


def solution(mesh):
    grid = Mesh(mesh.devices.reshape(CHIPS, CORES, PAIRS), ALL_AXES)
    rows = P(("chip", "core"), None)
    return jax.shard_map(
        on_device, mesh=grid, in_specs=(rows, rows, rows), out_specs=(rows, P()), check_vma=False
    )
```

```python
import math

import jax
import jax.numpy as jnp
from jax import lax
from jax.experimental import pallas as pl
from jax.experimental.pallas import tpu as pltpu
from jax.sharding import Mesh
from jax.sharding import PartitionSpec as P

WIDTH = 512
BASIS = 64
BLOCK = 512
HALF = BLOCK // 2
QUARTER = BLOCK // 4
DOCS = 32768
REACH = 5
CHUNK = 256
EXPONENT = -math.log(BLOCK / 4) / (2 * WIDTH) * math.log2(math.e)
UNLISTED = -1e30
CHIPS = 32
CORES = 2
PAIRS = 4
PARITIES = (0, 1, 1, 0)
HALVES = (0, 0, 1, 1)
NEAR = (1, -1)
FAR = (-2, 2)
ALL_AXES = ("chip", "core", "pairs")
NT = (((1,), (1,)), ((), ()))
EXACT = lax.Precision.HIGHEST


def move(array, reaches, sign):
    moves = []
    for chip in range(CHIPS):
        for core in range(CORES):
            for pair in range(PAIRS):
                to_chip = (chip + sign * reaches[PARITIES[pair]]) % CHIPS
                source = (chip * CORES + core) * PAIRS + pair
                target = (to_chip * CORES + core) * PAIRS + pair
                moves.append((source, target))
    return lax.ppermute(array, ALL_AXES, moves)


def swap_core(array):
    return lax.ppermute(array, "core", [(0, 1), (1, 0)])


def swap_parity(array):
    return lax.ppermute(array, "pairs", [(i, i ^ 1) for i in range(PAIRS)])


def swap_half(array):
    return lax.ppermute(array, "pairs", [(i, PAIRS - 1 - i) for i in range(PAIRS)])


def pack_kernel(place_ref, mask_ref, embeddings_ref, start_ref, full_out, half_out, start_out):
    half = place_ref[2]
    lane = lax.broadcasted_iota(jnp.int32, (16, WIDTH), 1)
    row = jnp.zeros((16, WIDTH), jnp.float32)
    for offset in range(REACH):
        row = jnp.where(lane == offset, mask_ref[0, offset].astype(jnp.float32), row)
    row = row.astype(jnp.bfloat16)
    full_out[:BLOCK, :] = embeddings_ref[...].astype(jnp.bfloat16)
    full_out[BLOCK:, :] = row
    sent = embeddings_ref[pl.ds(pl.multiple_of(half * HALF, HALF), HALF), :]
    half_out[:HALF, :] = sent.astype(jnp.bfloat16)
    half_out[HALF:, :] = row
    start_out[...] = start_ref[...].T


def column_bias(reach, own_mask, mate_mask, other_mask, core):
    lane = lax.broadcasted_iota(jnp.int32, (1, 128), 1)
    found = []
    for mask, row_core in ((own_mask, core), (mate_mask, 1 - core)):
        offset = 2 * reach + core - row_core
        ahead = jnp.where((lane == offset) & (lane < REACH), mask, 0.0)
        behind = jnp.where((lane == -offset) & (lane > 0) & (lane < REACH), other_mask, 0.0)
        flag = jnp.sum(ahead + behind, axis=1, keepdims=True)
        found.append(jnp.where(flag > 0, 0.0, UNLISTED))
    return found


def mask_row(ref):
    return ref[ref.shape[0] - 16 :, :128].astype(jnp.float32)[:1]


def norms(array):
    return EXPONENT * jnp.sum(jnp.square(array.astype(jnp.float32)), axis=1, keepdims=True)


def write_tiles(row_refs, biases, cols, out_ref):
    count = cols.shape[0]
    cols_sq = jnp.broadcast_to(norms(cols), (count, 128)).T[:1]
    for part, (row_ref, bias) in enumerate(zip(row_refs, biases)):
        shift = cols_sq + bias
        for first in range(0, BLOCK, CHUNK):
            rows = row_ref[first : first + CHUNK, :]
            inner = lax.dot_general(rows, cols, NT, preferred_element_type=jnp.float32)
            tile = jnp.exp2(inner * (-2.0 * EXPONENT) + norms(rows) + shift)
            start = part * BLOCK + first
            out_ref[start : start + CHUNK, :] = tile.astype(jnp.bfloat16)
    ones = jnp.ones((8, count), jnp.bfloat16)
    return lax.dot_general(ones, out_ref[...], NT, preferred_element_type=jnp.float32)[:1]


def near_kernel(place_ref, own_ref, mate_ref, near_ref, near_out, own_out, sum_out):
    core, parity, half = place_ref[0], place_ref[1], place_ref[2]
    reach = jnp.where(parity == 0, NEAR[0], NEAR[1])
    masks = mask_row(own_ref), mask_row(mate_ref)
    rows = (own_ref, mate_ref)
    start = pl.multiple_of((2 * half + parity) * QUARTER, QUARTER)
    bias = column_bias(0, *masks, masks[0], core)
    total = write_tiles(rows, bias, own_ref[pl.ds(start, QUARTER), :], own_out)
    bias = column_bias(reach, *masks, mask_row(near_ref), core)
    sum_out[...] = total + write_tiles(rows, bias, near_ref[:HALF, :], near_out)


def far_kernel(place_ref, own_ref, mate_ref, far_ref, sum_ref, far_out, sum_out):
    core, parity = place_ref[0], place_ref[1]
    reach = jnp.where(parity == 0, FAR[0], FAR[1])
    masks = mask_row(own_ref), mask_row(mate_ref)
    bias = column_bias(reach, *masks, mask_row(far_ref), core)
    rows = (own_ref, mate_ref)
    sum_out[...] = sum_ref[...] + write_tiles(rows, bias, far_ref[:HALF, :], far_out)


def multiply(vectors, far_ref, near_ref, own_ref, far_out, near_out, own_out):
    for weights_ref, out_ref in ((far_ref, far_out), (near_ref, near_out), (own_ref, own_out)):
        found = jnp.dot(vectors, weights_ref[...], preferred_element_type=jnp.float32)
        if found.shape[0] > BASIS:
            found = found[:BASIS] + found[BASIS:]
        out_ref[...] = found


def first_kernel(
    degree_ref, other_ref, own_start, mate_start, far, near, own, far_out, near_out, own_out, root_out
):
    root = lax.rsqrt(degree_ref[...] + other_ref[...])
    root_out[...] = root
    scaled = jnp.concatenate(
        [own_start[...] * root[:, :BLOCK], mate_start[...] * root[:, BLOCK:]], axis=1
    )
    multiply(scaled.astype(jnp.bfloat16), far, near, own, far_out, near_out, own_out)


def second_kernel(root_ref, own_ref, mate_ref, far, near, own, far_out, near_out, own_out):
    root = root_ref[...]
    scaled = jnp.concatenate([own_ref[...], mate_ref[...]], axis=1) * root * root
    high = scaled.astype(jnp.bfloat16)
    low = (scaled - high.astype(jnp.float32)).astype(jnp.bfloat16)
    multiply(jnp.concatenate([high, low]), far, near, own, far_out, near_out, own_out)


def products_kernel(root_ref, first_ref, second_ref, image_out, products_out):
    root = root_ref[:, :BLOCK]
    image = second_ref[...] * root
    image_out[...] = image
    both = jnp.concatenate([first_ref[...] * root, image])
    found = lax.dot_general(both, both, NT, precision=EXACT, preferred_element_type=jnp.float32)
    left = lax.broadcasted_iota(jnp.int32, (BASIS, 128), 1) < BASIS
    products_out[:BASIS, :] = jnp.where(left, found[:BASIS], found[BASIS:])
    products_out[BASIS:, :] = jnp.concatenate([found[:32, BASIS:], found[32:64, BASIS:]], axis=1)


def finish_kernel(products_ref, image_ref, basis_ref, projected_ref):
    work = products_ref[:BASIS, :] * (1.0 / DOCS)
    row = lax.broadcasted_iota(jnp.int32, (BASIS, 128), 0)
    lane = lax.broadcasted_iota(jnp.int32, (BASIS, 128), 1)
    left = lane < BASIS
    for j in range(BASIS):
        column = jnp.where(left, work[:, j : j + 1], work[:, BASIS + j : BASIS + j + 1])
        pivot_row = work[j : j + 1, :] + jnp.where(lane[:1] % BASIS == j, 1.0, 0.0)
        factor = jnp.where(row > j, column / column[j : j + 1, :], 0.0)
        work = work - factor * pivot_row
    diagonal = lane % BASIS == row
    pivots = jnp.where(diagonal, work, 0.0)
    scale = jnp.where(
        left,
        jnp.sum(pivots[:, :BASIS], axis=1, keepdims=True),
        jnp.sum(pivots[:, BASIS:], axis=1, keepdims=True),
    )
    inverse = jnp.where(diagonal, 1.0, jnp.where(lane % BASIS < row, work, 0.0)) * lax.rsqrt(scale)
    cross = jnp.concatenate([products_ref[BASIS:, :BASIS], products_ref[BASIS:, BASIS:]])
    first = inverse[:, :BASIS]
    half = jnp.dot(
        first, cross * (1.0 / DOCS), precision=EXACT, preferred_element_type=jnp.float32
    )
    projected_ref[...] = lax.dot_general(
        half, first, NT, precision=EXACT, preferred_element_type=jnp.float32
    )
    basis = jnp.dot(
        inverse[:, BASIS:], image_ref[...], precision=EXACT, preferred_element_type=jnp.float32
    )
    basis_ref[...] = basis.T


def call(kernel, outs, operands, scalars=0):
    vmem = pl.BlockSpec(memory_space=pltpu.VMEM)
    smem = pl.BlockSpec(memory_space=pltpu.SMEM)
    return pl.pallas_call(
        kernel,
        out_shape=[jax.ShapeDtypeStruct(shape, dtype) for shape, dtype in outs],
        in_specs=[smem] * scalars + [vmem] * (len(operands) - scalars),
        out_specs=[vmem] * len(outs),
        compiler_params=pltpu.CompilerParams(vmem_limit_bytes=32 * 2**20),
    )(*operands)


def on_device(embeddings, start_basis, pair_mask):
    f32, bf16 = jnp.float32, jnp.bfloat16
    wide = 2 * BLOCK
    core = lax.axis_index("core")
    pair = lax.axis_index("pairs")
    parity = jnp.where((pair == 1) | (pair == 2), 1, 0)
    half = jnp.where(pair >= 2, 1, 0)
    place = jnp.stack([core, parity, half]).astype(jnp.int32)

    packed, sent, own_start = call(
        pack_kernel,
        [((BLOCK + 16, WIDTH), bf16), ((HALF + 16, WIDTH), bf16), ((BASIS, BLOCK), f32)],
        (place, pair_mask, embeddings, start_basis),
        scalars=2,
    )
    far = move(sent, FAR, -1)
    near = move(sent, NEAR, -1)
    mate = swap_core(packed)
    mate_start = swap_core(own_start)
    near_weights, own_weights, sums = call(
        near_kernel,
        [((wide, HALF), bf16), ((wide, QUARTER), bf16), ((1, wide), f32)],
        (place, packed, mate, near),
        scalars=1,
    )
    far_weights, sums = call(
        far_kernel,
        [((wide, HALF), bf16), ((1, wide), f32)],
        (place, packed, mate, far, sums),
        scalars=1,
    )
    other = swap_core(sums)
    sums = sums + jnp.concatenate([other[:, BLOCK:], other[:, :BLOCK]], axis=1)
    sums = sums + swap_parity(sums)
    weights = (far_weights, near_weights, own_weights)
    terms = [((BASIS, HALF), f32), ((BASIS, HALF), f32), ((BASIS, QUARTER), f32)]

    def collect(far_term, near_term, own_term):
        total = move(far_term, FAR, 1) + move(near_term, NEAR, 1)
        blank = jnp.zeros_like(own_term)
        total = total + jnp.where(
            parity == 0,
            jnp.concatenate([own_term, blank], axis=1),
            jnp.concatenate([blank, own_term], axis=1),
        )
        total = total + swap_parity(total)
        other = swap_half(total)
        return jnp.where(
            half == 0,
            jnp.concatenate([total, other], axis=1),
            jnp.concatenate([other, total], axis=1),
        )

    far_term, near_term, own_term, root = call(
        first_kernel,
        terms + [((1, wide), f32)],
        (sums, swap_half(sums), own_start, mate_start, *weights),
    )
    first = collect(far_term, near_term, own_term)
    second = collect(*call(second_kernel, terms, (root, first, swap_core(first), *weights)))
    image, products = call(
        products_kernel, [((BASIS, BLOCK), f32), ((96, 128), f32)], (root, first, second)
    )
    products = products + swap_core(products)
    for bit in (1, 2, 4, 8, 16):
        other = lax.ppermute(products, "chip", [(i, i ^ bit) for i in range(CHIPS)])
        products = products + other
    return call(
        finish_kernel, [((BLOCK, BASIS), f32), ((BASIS, BASIS), f32)], (products, image)
    )


def solution(mesh):
    grid = Mesh(mesh.devices.reshape(CHIPS, CORES, PAIRS), ALL_AXES)
    rows = P(("chip", "core"), None)
    return jax.shard_map(
        on_device, mesh=grid, in_specs=(rows, rows, rows), out_specs=(rows, P()), check_vma=False
    )
```

```python
import functools
import math

import jax
import jax.numpy as jnp
from jax import lax
from jax.experimental import pallas as pl
from jax.experimental.pallas import tpu as pltpu
from jax.sharding import Mesh
from jax.sharding import PartitionSpec as P

WIDTH = 512
BASIS = 64
BLOCK = 512
HALF = BLOCK // 2
QUARTER = BLOCK // 4
DOCS = 32768
REACH = 5
CHUNK = 256
STEP = 8
EXPONENT = -math.log(BLOCK / 4) / (2 * WIDTH) * math.log2(math.e)
UNLISTED = -1e30
CHIPS = 32
CORES = 2
PAIRS = 4
PARITIES = (0, 1, 1, 0)
HALVES = (0, 0, 1, 1)
NEAR = (1, -1)
FAR = (-2, 2)
ALL_AXES = ("chip", "core", "pairs")
NT = (((1,), (1,)), ((), ()))
EXACT = lax.Precision.HIGHEST


def move(array, reaches, sign):
    moves = []
    for chip in range(CHIPS):
        for core in range(CORES):
            for pair in range(PAIRS):
                to_chip = (chip + sign * reaches[PARITIES[pair]]) % CHIPS
                source = (chip * CORES + core) * PAIRS + pair
                target = (to_chip * CORES + core) * PAIRS + pair
                moves.append((source, target))
    return lax.ppermute(array, ALL_AXES, moves)


def swap_core(array):
    return lax.ppermute(array, "core", [(0, 1), (1, 0)])


def other_chip(array, bits):
    return lax.ppermute(array, "chip", [(i, i ^ bits) for i in range(CHIPS)])


def other_planes(array):
    return [
        lax.ppermute(array, "pairs", [(i, step(i)) for i in range(PAIRS)])
        for step in (lambda i: i ^ 1, lambda i: PAIRS - 1 - i, lambda i: i ^ 2)
    ]


def place():
    pair = lax.axis_index("pairs")
    parity = jnp.where((pair == 1) | (pair == 2), 1, 0)
    return lax.axis_index("core"), parity, jnp.where(pair >= 2, 1, 0)


def pack_kernel(embeddings_ref, sent_ref, gate_ref, full_out):
    full_out[:BLOCK, :] = embeddings_ref[...].astype(jnp.bfloat16)
    full_out[BLOCK:, :] = sent_ref[HALF:, :]


def column_bias(reach, own_mask, mate_mask, other_mask, core):
    lane = lax.broadcasted_iota(jnp.int32, (1, 128), 1)
    found = []
    for mask, row_core in ((own_mask, core), (mate_mask, 1 - core)):
        offset = 2 * reach + core - row_core
        ahead = jnp.where((lane == offset) & (lane < REACH), mask, 0.0)
        behind = jnp.where((lane == -offset) & (lane > 0) & (lane < REACH), other_mask, 0.0)
        flag = jnp.sum(ahead + behind, axis=1, keepdims=True)
        found.append(jnp.where(flag > 0, 0.0, UNLISTED))
    return found


def mask_row(ref):
    return ref[ref.shape[0] - 16 :, :128].astype(jnp.float32)[:1]


def norms(array):
    return EXPONENT * jnp.sum(jnp.square(array.astype(jnp.float32)), axis=1, keepdims=True)


def write_tiles(row_refs, biases, cols, out_ref):
    count = cols.shape[0]
    cols_sq = jnp.broadcast_to(norms(cols), (count, 128)).T[:1]
    for part, (row_ref, bias) in enumerate(zip(row_refs, biases)):
        shift = cols_sq + bias
        for first in range(0, BLOCK, CHUNK):
            rows = row_ref[first : first + CHUNK, :]
            inner = lax.dot_general(rows, cols, NT, preferred_element_type=jnp.float32)
            tile = jnp.exp2(inner * (-2.0 * EXPONENT) + norms(rows) + shift)
            start = part * BLOCK + first
            out_ref[start : start + CHUNK, :] = tile.astype(jnp.bfloat16)
    ones = jnp.ones((8, count), jnp.bfloat16)
    return lax.dot_general(ones, out_ref[...], NT, preferred_element_type=jnp.float32)[:1]


def own_kernel(own_ref, mate_ref, own_out, sum_out):
    core, parity, half = place()
    masks = mask_row(own_ref), mask_row(mate_ref)
    bias = column_bias(0, *masks, masks[0], core)
    start = pl.multiple_of((2 * half + parity) * QUARTER, QUARTER)
    cols = own_ref[pl.ds(start, QUARTER), :]
    sum_out[...] = write_tiles((own_ref, mate_ref), bias, cols, own_out)


def reach_kernel(reaches, own_ref, mate_ref, reach_ref, sum_ref, tiles_out, sum_out):
    core, parity, _ = place()
    reach = jnp.where(parity == 0, reaches[0], reaches[1])
    masks = mask_row(own_ref), mask_row(mate_ref)
    bias = column_bias(reach, *masks, mask_row(reach_ref), core)
    rows = (own_ref, mate_ref)
    sum_out[...] = sum_ref[...] + write_tiles(rows, bias, reach_ref[:HALF, :], tiles_out)


def multiply(vectors, far_ref, near_ref, own_ref, far_out, near_out, own_out):
    for weights_ref, out_ref in ((far_ref, far_out), (near_ref, near_out), (own_ref, own_out)):
        found = jnp.dot(vectors, weights_ref[...], preferred_element_type=jnp.float32)
        if found.shape[0] > BASIS:
            found = found[:BASIS] + found[BASIS:]
        out_ref[...] = found


def first_kernel(
    sum_ref, same_ref, across_ref, both_ref, own_start, mate_start, far, near, own,
    far_out, near_out, own_out, root_out,
):
    degree = (sum_ref[...] + same_ref[...]) + (across_ref[...] + both_ref[...])
    root = lax.rsqrt(degree)
    root_out[...] = root
    scaled = jnp.concatenate(
        [own_start[...] * root[:, :BLOCK], mate_start[...] * root[:, BLOCK:]], axis=1
    )
    multiply(scaled.astype(jnp.bfloat16), far, near, own, far_out, near_out, own_out)


def second_kernel(root_ref, own_ref, mate_ref, far, near, own, far_out, near_out, own_out):
    root = root_ref[...]
    scaled = jnp.concatenate([own_ref[...], mate_ref[...]], axis=1) * root * root
    high = scaled.astype(jnp.bfloat16)
    low = (scaled - high.astype(jnp.float32)).astype(jnp.bfloat16)
    multiply(jnp.concatenate([high, low]), far, near, own, far_out, near_out, own_out)


def products_kernel(root_ref, first_ref, second_ref, image_out, products_out):
    root = root_ref[:, :BLOCK]
    image = second_ref[...] * root
    image_out[...] = image
    both = jnp.concatenate([first_ref[...] * root, image])
    found = lax.dot_general(both, both, NT, precision=EXACT, preferred_element_type=jnp.float32)
    row = lax.broadcasted_iota(jnp.int32, (BASIS, BASIS), 0)
    lane = lax.broadcasted_iota(jnp.int32, (BASIS, BASIS), 1)
    gram = found[BASIS:, BASIS:]
    square = jnp.where(row >= lane, found[:BASIS, :BASIS], gram)
    diagonal = jnp.sum(jnp.where(row == lane, gram, 0.0), axis=0, keepdims=True)
    products_out[:BASIS, :] = jnp.concatenate([square, found[:BASIS, BASIS:]], axis=1)
    products_out[BASIS:, :] = jnp.broadcast_to(
        jnp.concatenate([diagonal, diagonal], axis=1), (8, 2 * BASIS)
    )


def finish_kernel(products_ref, image_ref, basis_ref, projected_ref):
    square = products_ref[:BASIS, :BASIS]
    turned = square.T
    row = lax.broadcasted_iota(jnp.int32, (BASIS, BASIS), 0)
    lane = lax.broadcasted_iota(jnp.int32, (BASIS, BASIS), 1)
    first = jnp.where(row >= lane, square, turned)
    second = jnp.where(row > lane, turned, square)
    second = jnp.where(row == lane, products_ref[BASIS : BASIS + 1, :BASIS], second)
    work = jnp.concatenate([first, second], axis=1) * (1.0 / DOCS)
    row = lax.broadcasted_iota(jnp.int32, (BASIS, 128), 0)
    lane = lax.broadcasted_iota(jnp.int32, (BASIS, 128), 1)
    left = lane < BASIS
    for start in range(0, BASIS, STEP):
        columns = [
            jnp.take_along_axis(work, jnp.where(left, j, BASIS + j), axis=1)
            for j in range(start, start + STEP)
        ]
        rows = [work[j : j + 1, :] for j in range(start, start + STEP)]
        for k in range(STEP):
            j = start + k
            factor = jnp.where(row > j, columns[k] * (1.0 / columns[k][j : j + 1, :]), 0.0)
            pivot_row = rows[k] + jnp.where(lane[:1] % BASIS == j, 1.0, 0.0)
            for later in range(k + 1, STEP):
                columns[later] = columns[later] - factor * columns[later][j : j + 1, :]
                rows[later] = rows[later] - factor[start + later : start + later + 1, :] * pivot_row
            work = work - factor * pivot_row
    diagonal = lane % BASIS == row
    pivots = jnp.where(diagonal, work, 0.0)
    scale = jnp.where(
        left,
        jnp.sum(pivots[:, :BASIS], axis=1, keepdims=True),
        jnp.sum(pivots[:, BASIS:], axis=1, keepdims=True),
    )
    inverse = jnp.where(diagonal, 1.0, jnp.where(lane % BASIS < row, work, 0.0)) * lax.rsqrt(scale)
    cross = products_ref[:BASIS, BASIS:]
    first = inverse[:, :BASIS]
    half = jnp.dot(
        first, cross * (1.0 / DOCS), precision=EXACT, preferred_element_type=jnp.float32
    )
    projected_ref[...] = lax.dot_general(
        half, first, NT, precision=EXACT, preferred_element_type=jnp.float32
    )
    basis_ref[...] = jnp.dot(
        inverse[:, BASIS:], image_ref[...], precision=EXACT, preferred_element_type=jnp.float32
    )


def call(kernel, outs, operands, scratch=(), far_operands=0):
    spaces = [pl.ANY] * far_operands + [pltpu.VMEM] * (len(operands) - far_operands)
    limit = None if far_operands else 32 * 2**20
    return pl.pallas_call(
        kernel,
        out_shape=[jax.ShapeDtypeStruct(shape, dtype) for shape, dtype in outs],
        in_specs=[pl.BlockSpec(memory_space=space) for space in spaces],
        out_specs=[pl.BlockSpec(memory_space=pltpu.VMEM)] * len(outs),
        scratch_shapes=scratch,
        compiler_params=pltpu.CompilerParams(vmem_limit_bytes=limit),
    )(*operands)


def on_device(embeddings, start_basis, pair_mask):
    f32, bf16 = jnp.float32, jnp.bfloat16
    wide = 2 * BLOCK
    _, parity, half = place()

    own_start = start_basis.T
    mate_start = swap_core(own_start)
    rows = lax.dynamic_slice_in_dim(embeddings, half * HALF, HALF, 0).astype(bf16)
    mask = jnp.pad(pair_mask.astype(bf16), ((HALF, 15), (0, WIDTH - REACH)))
    sent = jnp.pad(rows, ((0, 16), (0, 0))) + mask
    far = move(sent, FAR, -1)
    (packed,) = call(
        pack_kernel, [((BLOCK + 16, WIDTH), bf16)], (embeddings, sent, mate_start)
    )
    mate = swap_core(packed)
    near = move(sent, NEAR, -1)
    tiles = [((wide, HALF), bf16), ((1, wide), f32)]
    own_weights, sums = call(
        own_kernel, [((wide, QUARTER), bf16), ((1, wide), f32)], (packed, mate)
    )
    far_kernel = functools.partial(reach_kernel, FAR)
    near_kernel = functools.partial(reach_kernel, NEAR)
    far_weights, sums = call(far_kernel, tiles, (packed, mate, far, sums))
    near_weights, sums = call(near_kernel, tiles, (packed, mate, near, sums))
    other = swap_core(sums)
    sums = sums + jnp.concatenate([other[:, BLOCK:], other[:, :BLOCK]], axis=1)
    plane_sums = [sums, *other_planes(sums)]
    weights = (far_weights, near_weights, own_weights)
    terms = [((BASIS, HALF), f32), ((BASIS, HALF), f32), ((BASIS, QUARTER), f32)]

    def collect(far_term, near_term, own_term):
        total = move(far_term, FAR, 1) + move(near_term, NEAR, 1)
        blank = jnp.zeros_like(own_term)
        total = total + jnp.where(
            parity == 0,
            jnp.concatenate([own_term, blank], axis=1),
            jnp.concatenate([blank, own_term], axis=1),
        )
        same, across, both = other_planes(total)
        total = total + same
        other = across + both
        return jnp.where(
            half == 0,
            jnp.concatenate([total, other], axis=1),
            jnp.concatenate([other, total], axis=1),
        )

    far_term, near_term, own_term, root = call(
        first_kernel,
        terms + [((1, wide), f32)],
        (*plane_sums, own_start, mate_start, *weights),
    )
    first = collect(far_term, near_term, own_term)
    second = collect(*call(second_kernel, terms, (root, first, swap_core(first), *weights)))
    image, products = call(
        products_kernel, [((BASIS, BLOCK), f32), ((BASIS + 8, 128), f32)], (root, first, second)
    )
    products = products + swap_core(products)
    for bits in (1, 2, 7, 8, 24):
        products = products + other_chip(products, bits)
    basis, projected = call(
        finish_kernel, [((BASIS, BLOCK), f32), ((BASIS, BASIS), f32)], (products, image)
    )
    return basis.T, projected


def solution(mesh):
    grid = Mesh(mesh.devices.reshape(CHIPS, CORES, PAIRS), ALL_AXES)
    rows = P(("chip", "core"), None)
    return jax.shard_map(
        on_device, mesh=grid, in_specs=(rows, rows, rows), out_specs=(rows, P()), check_vma=False
    )
```

```python
import functools
import math

import jax
import jax.numpy as jnp
from jax import lax
from jax.experimental import pallas as pl
from jax.experimental.pallas import tpu as pltpu
from jax.sharding import Mesh
from jax.sharding import PartitionSpec as P

WIDTH = 512
BASIS = 64
BLOCK = 512
HALF = BLOCK // 2
QUARTER = BLOCK // 4
DOCS = 32768
REACH = 5
CHUNK = 256
STEP = 8
EXPONENT = -math.log(BLOCK / 4) / (2 * WIDTH) * math.log2(math.e)
UNLISTED = -1e30
CHIPS = 32
CORES = 2
PAIRS = 4
PARITIES = (0, 1, 1, 0)
HALVES = (0, 0, 1, 1)
NEAR = (1, -1)
FAR = (-2, 2)
ALL_AXES = ("chip", "core", "pairs")
NT = (((1,), (1,)), ((), ()))
EXACT = lax.Precision.HIGHEST


def move(array, reaches, sign):
    moves = []
    for chip in range(CHIPS):
        for core in range(CORES):
            for pair in range(PAIRS):
                to_chip = (chip + sign * reaches[PARITIES[pair]]) % CHIPS
                source = (chip * CORES + core) * PAIRS + pair
                target = (to_chip * CORES + core) * PAIRS + pair
                moves.append((source, target))
    return lax.ppermute(array, ALL_AXES, moves)


def swap_core(array):
    return lax.ppermute(array, "core", [(0, 1), (1, 0)])


def other_chip(array, bits, core_bit=0):
    count = CHIPS * CORES
    return lax.ppermute(
        array, ("chip", "core"), [(i, i ^ (CORES * bits + core_bit)) for i in range(count)]
    )


def other_planes(array):
    return [
        lax.ppermute(array, "pairs", [(i, step(i)) for i in range(PAIRS)])
        for step in (lambda i: i ^ 1, lambda i: PAIRS - 1 - i, lambda i: i ^ 2)
    ]


def place():
    pair = lax.axis_index("pairs")
    parity = jnp.where((pair == 1) | (pair == 2), 1, 0)
    return lax.axis_index("core"), parity, jnp.where(pair >= 2, 1, 0)


def pack_kernel(embeddings_ref, sent_ref, gate_ref, full_out):
    full_out[:BLOCK, :] = embeddings_ref[...].astype(jnp.bfloat16)
    full_out[BLOCK:, :] = sent_ref[HALF:, :]


def column_bias(reach, own_mask, mate_mask, other_mask, core):
    lane = lax.broadcasted_iota(jnp.int32, (1, 128), 1)
    found = []
    for mask, row_core in ((own_mask, core), (mate_mask, 1 - core)):
        offset = 2 * reach + core - row_core
        ahead = jnp.where((lane == offset) & (lane < REACH), mask, 0.0)
        behind = jnp.where((lane == -offset) & (lane > 0) & (lane < REACH), other_mask, 0.0)
        flag = jnp.sum(ahead + behind, axis=1, keepdims=True)
        found.append(jnp.where(flag > 0, 0.0, UNLISTED))
    return found


def mask_row(ref):
    return ref[ref.shape[0] - 16 :, :128].astype(jnp.float32)[:1]


def norms(array):
    return EXPONENT * jnp.sum(jnp.square(array.astype(jnp.float32)), axis=1, keepdims=True)


def write_tiles(row_refs, biases, cols, out_ref):
    count = cols.shape[0]
    cols_sq = jnp.broadcast_to(norms(cols), (count, 128)).T[:1]
    for part, (row_ref, bias) in enumerate(zip(row_refs, biases)):
        shift = cols_sq + bias
        for first in range(0, BLOCK, CHUNK):
            rows = row_ref[first : first + CHUNK, :]
            inner = lax.dot_general(rows, cols, NT, preferred_element_type=jnp.float32)
            tile = jnp.exp2(inner * (-2.0 * EXPONENT) + norms(rows) + shift)
            start = part * BLOCK + first
            out_ref[start : start + CHUNK, :] = tile.astype(jnp.bfloat16)
    ones = jnp.ones((8, count), jnp.bfloat16)
    return lax.dot_general(ones, out_ref[...], NT, preferred_element_type=jnp.float32)[:1]


def own_kernel(own_ref, mate_ref, own_out, sum_out):
    core, parity, half = place()
    masks = mask_row(own_ref), mask_row(mate_ref)
    bias = column_bias(0, *masks, masks[0], core)
    start = pl.multiple_of((2 * half + parity) * QUARTER, QUARTER)
    cols = own_ref[pl.ds(start, QUARTER), :]
    sum_out[...] = write_tiles((own_ref, mate_ref), bias, cols, own_out)


def reach_kernel(
    reaches, own_ref, mate_ref, reach_ref, sum_ref, tiles_out, sum_out, *turned_out
):
    core, parity, _ = place()
    reach = jnp.where(parity == 0, reaches[0], reaches[1])
    masks = mask_row(own_ref), mask_row(mate_ref)
    bias = column_bias(reach, *masks, mask_row(reach_ref), core)
    rows = (own_ref, mate_ref)
    total = sum_ref[...] + write_tiles(rows, bias, reach_ref[:HALF, :], tiles_out)
    sum_out[...] = total
    for out_ref in turned_out:
        out_ref[...] = jnp.concatenate([total[:, BLOCK:], total[:, :BLOCK]], axis=1)


def multiply(vectors, far_ref, near_ref, own_ref, far_out, near_out, own_out):
    for weights_ref, out_ref in ((far_ref, far_out), (near_ref, near_out), (own_ref, own_out)):
        found = jnp.dot(vectors, weights_ref[...], preferred_element_type=jnp.float32)
        if found.shape[0] > BASIS:
            found = found[:BASIS] + found[BASIS:]
        out_ref[...] = found


def first_kernel(
    sum_ref, same_ref, across_ref, both_ref, own_start, mate_start, far, near, own,
    far_out, near_out, own_out, root_out,
):
    degree = (sum_ref[...] + same_ref[...]) + (across_ref[...] + both_ref[...])
    root = lax.rsqrt(degree)
    root_out[...] = root
    scaled = jnp.concatenate(
        [own_start[...] * root[:, :BLOCK], mate_start[...] * root[:, BLOCK:]], axis=1
    )
    multiply(scaled.astype(jnp.bfloat16), far, near, own, far_out, near_out, own_out)


def second_kernel(root_ref, own_ref, mate_ref, far, near, own, far_out, near_out, own_out):
    root = root_ref[...]
    scaled = jnp.concatenate([own_ref[...], mate_ref[...]], axis=1) * root * root
    high = scaled.astype(jnp.bfloat16)
    low = (scaled - high.astype(jnp.float32)).astype(jnp.bfloat16)
    multiply(jnp.concatenate([high, low]), far, near, own, far_out, near_out, own_out)


def products_kernel(root_ref, first_ref, second_ref, image_out, products_out):
    root = root_ref[:, :BLOCK]
    image = second_ref[...] * root
    image_out[...] = image
    both = jnp.concatenate([first_ref[...] * root, image])
    found = lax.dot_general(both, both, NT, precision=EXACT, preferred_element_type=jnp.float32)
    row = lax.broadcasted_iota(jnp.int32, (BASIS, BASIS), 0)
    lane = lax.broadcasted_iota(jnp.int32, (BASIS, BASIS), 1)
    gram = found[BASIS:, BASIS:]
    square = jnp.where(row >= lane, found[:BASIS, :BASIS], gram)
    diagonal = jnp.sum(jnp.where(row == lane, gram, 0.0), axis=0, keepdims=True)
    products_out[:BASIS, :] = jnp.concatenate([square, found[:BASIS, BASIS:]], axis=1)
    products_out[BASIS:, :] = jnp.broadcast_to(
        jnp.concatenate([diagonal, diagonal], axis=1), (8, 2 * BASIS)
    )


def finish_kernel(products_ref, image_ref, basis_ref, projected_ref):
    square = products_ref[:BASIS, :BASIS]
    turned = square.T
    row = lax.broadcasted_iota(jnp.int32, (BASIS, BASIS), 0)
    lane = lax.broadcasted_iota(jnp.int32, (BASIS, BASIS), 1)
    first = jnp.where(row >= lane, square, turned)
    second = jnp.where(row > lane, turned, square)
    second = jnp.where(row == lane, products_ref[BASIS : BASIS + 1, :BASIS], second)
    work = jnp.concatenate([first, second], axis=1) * (1.0 / DOCS)
    row = lax.broadcasted_iota(jnp.int32, (BASIS, 128), 0)
    lane = lax.broadcasted_iota(jnp.int32, (BASIS, 128), 1)
    left = lane < BASIS
    for start in range(0, BASIS, STEP):
        columns = [
            jnp.take_along_axis(work, jnp.where(left, j, BASIS + j), axis=1)
            for j in range(start, start + STEP)
        ]
        rows = [work[j : j + 1, :] for j in range(start, start + STEP)]
        for k in range(STEP):
            j = start + k
            factor = jnp.where(row > j, columns[k] * (1.0 / columns[k][j : j + 1, :]), 0.0)
            pivot_row = rows[k] + jnp.where(lane[:1] % BASIS == j, 1.0, 0.0)
            for later in range(k + 1, STEP):
                columns[later] = columns[later] - factor * columns[later][j : j + 1, :]
                rows[later] = rows[later] - factor[start + later : start + later + 1, :] * pivot_row
            work = work - factor * pivot_row
    diagonal = lane % BASIS == row
    pivots = jnp.where(diagonal, work, 0.0)
    scale = jnp.where(
        left,
        jnp.sum(pivots[:, :BASIS], axis=1, keepdims=True),
        jnp.sum(pivots[:, BASIS:], axis=1, keepdims=True),
    )
    inverse = jnp.where(diagonal, 1.0, jnp.where(lane % BASIS < row, work, 0.0)) * lax.rsqrt(scale)
    cross = products_ref[:BASIS, BASIS:]
    first = inverse[:, :BASIS]
    half = jnp.dot(
        first, cross * (1.0 / DOCS), precision=EXACT, preferred_element_type=jnp.float32
    )
    projected_ref[...] = lax.dot_general(
        half, first, NT, precision=EXACT, preferred_element_type=jnp.float32
    )
    basis_ref[...] = jnp.dot(
        inverse[:, BASIS:], image_ref[...], precision=EXACT, preferred_element_type=jnp.float32
    )


def call(kernel, outs, operands, scratch=(), far_operands=0):
    spaces = [pl.ANY] * far_operands + [pltpu.VMEM] * (len(operands) - far_operands)
    limit = None if far_operands else 32 * 2**20
    return pl.pallas_call(
        kernel,
        out_shape=[jax.ShapeDtypeStruct(shape, dtype) for shape, dtype in outs],
        in_specs=[pl.BlockSpec(memory_space=space) for space in spaces],
        out_specs=[pl.BlockSpec(memory_space=pltpu.VMEM)] * len(outs),
        scratch_shapes=scratch,
        compiler_params=pltpu.CompilerParams(vmem_limit_bytes=limit),
    )(*operands)


def on_device(embeddings, start_basis, pair_mask):
    f32, bf16 = jnp.float32, jnp.bfloat16
    wide = 2 * BLOCK
    _, parity, half = place()

    own_start = start_basis.T
    mate_start = swap_core(own_start)
    rows = lax.dynamic_slice_in_dim(embeddings, half * HALF, HALF, 0).astype(bf16)
    mask = jnp.pad(pair_mask.astype(bf16), ((HALF, 15), (0, WIDTH - REACH)))
    sent = jnp.pad(rows, ((0, 16), (0, 0))) + mask
    far = move(sent, FAR, -1)
    (packed,) = call(
        pack_kernel, [((BLOCK + 16, WIDTH), bf16)], (embeddings, sent, mate_start)
    )
    mate = swap_core(packed)
    near = move(sent, NEAR, -1)
    tiles = [((wide, HALF), bf16), ((1, wide), f32), ((1, wide), f32)]
    own_weights, sums = call(
        own_kernel, [((wide, QUARTER), bf16), ((1, wide), f32)], (packed, mate)
    )
    far_kernel = functools.partial(reach_kernel, FAR)
    near_kernel = functools.partial(reach_kernel, NEAR)
    far_weights, sums = call(far_kernel, tiles[:2], (packed, mate, far, sums))
    near_weights, sums, turned = call(near_kernel, tiles, (packed, mate, near, sums))
    sums = sums + swap_core(turned)
    plane_sums = [sums, *other_planes(sums)]
    weights = (far_weights, near_weights, own_weights)
    terms = [((BASIS, HALF), f32), ((BASIS, HALF), f32), ((BASIS, QUARTER), f32)]

    def collect(far_term, near_term, own_term):
        total = move(far_term, FAR, 1) + move(near_term, NEAR, 1)
        blank = jnp.zeros_like(own_term)
        total = total + jnp.where(
            parity == 0,
            jnp.concatenate([own_term, blank], axis=1),
            jnp.concatenate([blank, own_term], axis=1),
        )
        same, across, both = other_planes(total)
        total = total + same
        other = across + both
        return jnp.where(
            half == 0,
            jnp.concatenate([total, other], axis=1),
            jnp.concatenate([other, total], axis=1),
        )

    far_term, near_term, own_term, root = call(
        first_kernel,
        terms + [((1, wide), f32)],
        (*plane_sums, own_start, mate_start, *weights),
    )
    first = collect(far_term, near_term, own_term)
    second = collect(*call(second_kernel, terms, (root, first, swap_core(first), *weights)))
    image, products = call(
        products_kernel, [((BASIS, BLOCK), f32), ((BASIS + 8, 128), f32)], (root, first, second)
    )
    for group in ((8, 24, 16), (1, 2, 3)):
        one, two, three = [other_chip(products, bits) for bits in group]
        products = (products + one) + (two + three)
    mate_products = swap_core(products)
    one, two = other_chip(products, 7), other_chip(products, 7, 1)
    products = (products + mate_products) + (one + two)
    basis, projected = call(
        finish_kernel, [((BASIS, BLOCK), f32), ((BASIS, BASIS), f32)], (products, image)
    )
    return basis.T, projected


def solution(mesh):
    grid = Mesh(mesh.devices.reshape(CHIPS, CORES, PAIRS), ALL_AXES)
    rows = P(("chip", "core"), None)
    return jax.shard_map(
        on_device, mesh=grid, in_specs=(rows, rows, rows), out_specs=(rows, P()), check_vma=False
    )
```

```python
import functools
import math

import jax
import jax.numpy as jnp
from jax import lax
from jax.experimental import pallas as pl
from jax.experimental.pallas import tpu as pltpu
from jax.sharding import Mesh
from jax.sharding import PartitionSpec as P

WIDTH = 512
BASIS = 64
BLOCK = 512
HALF = BLOCK // 2
QUARTER = BLOCK // 4
DOCS = 32768
REACH = 5
CHUNK = 256
STEP = 8
PIECE = 64
MAIN = 192
EXPONENT = -math.log(BLOCK / 4) / (2 * WIDTH) * math.log2(math.e)
UNLISTED = -1e30
CHIPS = 32
CORES = 2
PAIRS = 4
PARITIES = (0, 1, 1, 0)
HALVES = (0, 0, 1, 1)
NEAR = (1, -1)
FAR = (-2, 2)
ALL_AXES = ("chip", "core", "pairs")
NT = (((1,), (1,)), ((), ()))
EXACT = lax.Precision.HIGHEST


def move(array, reaches, sign, across=0):
    moves = []
    for chip in range(CHIPS):
        for core in range(CORES):
            for pair in range(PAIRS):
                to_pair = pair ^ across
                to_chip = (chip + sign * reaches[PARITIES[to_pair]]) % CHIPS
                source = (chip * CORES + core) * PAIRS + pair
                target = (to_chip * CORES + core) * PAIRS + to_pair
                moves.append((source, target))
    return lax.ppermute(array, ALL_AXES, moves)


def swap_core(array):
    return lax.ppermute(array, "core", [(0, 1), (1, 0)])


def other_chip(array, bits, core_bit=0):
    count = CHIPS * CORES
    return lax.ppermute(
        array, ("chip", "core"), [(i, i ^ (CORES * bits + core_bit)) for i in range(count)]
    )


def other_planes(array):
    return [
        lax.ppermute(array, "pairs", [(i, step(i)) for i in range(PAIRS)])
        for step in (lambda i: i ^ 1, lambda i: PAIRS - 1 - i, lambda i: i ^ 2)
    ]


def place():
    pair = lax.axis_index("pairs")
    parity = jnp.where((pair == 1) | (pair == 2), 1, 0)
    return lax.axis_index("core"), parity, jnp.where(pair >= 2, 1, 0)


def mask_rows(mask_ref):
    lane = lax.broadcasted_iota(jnp.int32, (16, WIDTH), 1)
    row = jnp.zeros((16, WIDTH), jnp.float32)
    for offset in range(REACH):
        row = jnp.where(lane == offset, mask_ref[0, offset].astype(jnp.float32), row)
    return row.astype(jnp.bfloat16)


def send_kernel(
    mask_ref, embeddings_ref, main_out, rest_out, sent_out, full_out,
    mask, rows, mask_arrived, rows_arrived,
):
    half = place()[2]
    mask_copy = pltpu.make_async_copy(mask_ref, mask, mask_arrived)
    mask_copy.start()
    pieces = HALF // PIECE
    copies = []
    for part in range(2 * pieces):
        which = half if part < pieces else 1 - half
        first = pl.multiple_of(which * HALF + part % pieces * PIECE, PIECE)
        source = embeddings_ref.at[pl.ds(first, PIECE), :]
        copies.append((first, pltpu.make_async_copy(source, rows.at[part], rows_arrived.at[part])))
        copies[-1][1].start()
    for part, (place_in_block, copy) in enumerate(copies):
        copy.wait()
        first = part * PIECE
        piece = rows[part].astype(jnp.bfloat16)
        full_out[pl.ds(place_in_block, PIECE), :] = piece
        if part < pieces:
            sent_out[first : first + PIECE, :] = piece
            if first < MAIN:
                main_out[first : first + PIECE, :] = piece
            else:
                rest_out[first - MAIN : first - MAIN + PIECE, :] = piece
    mask_copy.wait()
    row = mask_rows(mask)
    sent_out[HALF:, :] = row
    main_out[MAIN:, :] = row
    full_out[BLOCK:, :] = row


def column_bias(reach, own_mask, mate_mask, other_mask, core):
    lane = lax.broadcasted_iota(jnp.int32, (1, 128), 1)
    found = []
    for mask, row_core in ((own_mask, core), (mate_mask, 1 - core)):
        offset = 2 * reach + core - row_core
        ahead = jnp.where((lane == offset) & (lane < REACH), mask, 0.0)
        behind = jnp.where((lane == -offset) & (lane > 0) & (lane < REACH), other_mask, 0.0)
        flag = jnp.sum(ahead + behind, axis=1, keepdims=True)
        found.append(jnp.where(flag > 0, 0.0, UNLISTED))
    return found


def mask_row(ref):
    return ref[ref.shape[0] - 16 :, :128].astype(jnp.float32)[:1]


def norms(array):
    return EXPONENT * jnp.sum(jnp.square(array.astype(jnp.float32)), axis=1, keepdims=True)


def write_tiles(row_refs, biases, cols, out_ref):
    count = cols.shape[0]
    cols_sq = jnp.broadcast_to(norms(cols), (count, 128)).T[:1]
    for part, (row_ref, bias) in enumerate(zip(row_refs, biases)):
        shift = cols_sq + bias
        for first in range(0, BLOCK, CHUNK):
            rows = row_ref[first : first + CHUNK, :]
            inner = lax.dot_general(rows, cols, NT, preferred_element_type=jnp.float32)
            tile = jnp.exp2(inner * (-2.0 * EXPONENT) + norms(rows) + shift)
            start = part * BLOCK + first
            out_ref[start : start + CHUNK, :] = tile.astype(jnp.bfloat16)
    ones = jnp.ones((8, count), jnp.bfloat16)
    return lax.dot_general(ones, out_ref[...], NT, preferred_element_type=jnp.float32)[:1]


def own_kernel(own_ref, mate_ref, own_out, sum_out):
    core, parity, half = place()
    masks = mask_row(own_ref), mask_row(mate_ref)
    bias = column_bias(0, *masks, masks[0], core)
    start = pl.multiple_of((2 * half + parity) * QUARTER, QUARTER)
    cols = own_ref[pl.ds(start, QUARTER), :]
    sum_out[...] = write_tiles((own_ref, mate_ref), bias, cols, own_out)


def reach_kernel(reaches, count, own_ref, mate_ref, *refs):
    parts, (sum_ref, tiles_out, sum_out, *turned_out) = refs[:count], refs[count:]
    core, parity, _ = place()
    reach = jnp.where(parity == 0, reaches[0], reaches[1])
    masks = mask_row(own_ref), mask_row(mate_ref)
    bias = column_bias(reach, *masks, mask_row(parts[0]), core)
    cols = [parts[0][: parts[0].shape[0] - 16, :]] + [ref[...] for ref in parts[1:]]
    cols = jnp.concatenate(cols) if count > 1 else cols[0]
    total = sum_ref[...] + write_tiles((own_ref, mate_ref), bias, cols, tiles_out)
    sum_out[...] = total
    for out_ref in turned_out:
        out_ref[...] = jnp.concatenate([total[:, BLOCK:], total[:, :BLOCK]], axis=1)


def multiply(vectors, far_ref, near_ref, own_ref, far_out, near_out, own_out):
    for weights_ref, out_ref in ((far_ref, far_out), (near_ref, near_out), (own_ref, own_out)):
        found = jnp.dot(vectors, weights_ref[...], preferred_element_type=jnp.float32)
        if found.shape[0] > BASIS:
            found = found[:BASIS] + found[BASIS:]
        out_ref[...] = found


def first_kernel(
    sum_ref, same_ref, across_ref, both_ref, own_start, mate_start, far, near, own,
    far_out, near_out, own_out, root_out,
):
    degree = (sum_ref[...] + same_ref[...]) + (across_ref[...] + both_ref[...])
    root = lax.rsqrt(degree)
    root_out[...] = root
    scaled = jnp.concatenate(
        [own_start[...] * root[:, :BLOCK], mate_start[...] * root[:, BLOCK:]], axis=1
    )
    multiply(scaled.astype(jnp.bfloat16), far, near, own, far_out, near_out, own_out)


def second_kernel(root_ref, own_ref, mate_ref, far, near, own, far_out, near_out, own_out):
    root = root_ref[...]
    scaled = jnp.concatenate([own_ref[...], mate_ref[...]], axis=1) * root * root
    high = scaled.astype(jnp.bfloat16)
    low = (scaled - high.astype(jnp.float32)).astype(jnp.bfloat16)
    multiply(jnp.concatenate([high, low]), far, near, own, far_out, near_out, own_out)


def products_kernel(root_ref, first_ref, second_ref, image_out, products_out):
    root = root_ref[:, :BLOCK]
    image = second_ref[...] * root
    image_out[...] = image
    both = jnp.concatenate([first_ref[...] * root, image])
    found = lax.dot_general(both, both, NT, precision=EXACT, preferred_element_type=jnp.float32)
    row = lax.broadcasted_iota(jnp.int32, (BASIS, BASIS), 0)
    lane = lax.broadcasted_iota(jnp.int32, (BASIS, BASIS), 1)
    gram = found[BASIS:, BASIS:]
    square = jnp.where(row >= lane, found[:BASIS, :BASIS], gram)
    diagonal = jnp.sum(jnp.where(row == lane, gram, 0.0), axis=0, keepdims=True)
    products_out[:BASIS, :] = jnp.concatenate([square, found[:BASIS, BASIS:]], axis=1)
    products_out[BASIS:, :] = jnp.broadcast_to(
        jnp.concatenate([diagonal, diagonal], axis=1), (8, 2 * BASIS)
    )


def finish_kernel(products_ref, image_ref, basis_ref, projected_ref):
    square = products_ref[:BASIS, :BASIS]
    turned = square.T
    row = lax.broadcasted_iota(jnp.int32, (BASIS, BASIS), 0)
    lane = lax.broadcasted_iota(jnp.int32, (BASIS, BASIS), 1)
    first = jnp.where(row >= lane, square, turned)
    second = jnp.where(row > lane, turned, square)
    second = jnp.where(row == lane, products_ref[BASIS : BASIS + 1, :BASIS], second)
    work = jnp.concatenate([first, second], axis=1) * (1.0 / DOCS)
    row = lax.broadcasted_iota(jnp.int32, (BASIS, 128), 0)
    lane = lax.broadcasted_iota(jnp.int32, (BASIS, 128), 1)
    left = lane < BASIS
    for start in range(0, BASIS, STEP):
        columns = [
            jnp.take_along_axis(work, jnp.where(left, j, BASIS + j), axis=1)
            for j in range(start, start + STEP)
        ]
        rows = [work[j : j + 1, :] for j in range(start, start + STEP)]
        for k in range(STEP):
            j = start + k
            factor = jnp.where(row > j, columns[k] * (1.0 / columns[k][j : j + 1, :]), 0.0)
            pivot_row = rows[k] + jnp.where(lane[:1] % BASIS == j, 1.0, 0.0)
            for later in range(k + 1, STEP):
                columns[later] = columns[later] - factor * columns[later][j : j + 1, :]
                rows[later] = rows[later] - factor[start + later : start + later + 1, :] * pivot_row
            work = work - factor * pivot_row
    diagonal = lane % BASIS == row
    pivots = jnp.where(diagonal, work, 0.0)
    scale = jnp.where(
        left,
        jnp.sum(pivots[:, :BASIS], axis=1, keepdims=True),
        jnp.sum(pivots[:, BASIS:], axis=1, keepdims=True),
    )
    inverse = jnp.where(diagonal, 1.0, jnp.where(lane % BASIS < row, work, 0.0)) * lax.rsqrt(scale)
    cross = products_ref[:BASIS, BASIS:]
    first = inverse[:, :BASIS]
    half = jnp.dot(
        first, cross * (1.0 / DOCS), precision=EXACT, preferred_element_type=jnp.float32
    )
    projected_ref[...] = lax.dot_general(
        half, first, NT, precision=EXACT, preferred_element_type=jnp.float32
    )
    basis_ref[...] = jnp.dot(
        inverse[:, BASIS:], image_ref[...], precision=EXACT, preferred_element_type=jnp.float32
    )


def call(kernel, outs, operands, scratch=(), far_operands=0):
    spaces = [pl.ANY] * far_operands + [pltpu.VMEM] * (len(operands) - far_operands)
    limit = None if far_operands else 32 * 2**20
    return pl.pallas_call(
        kernel,
        out_shape=[jax.ShapeDtypeStruct(shape, dtype) for shape, dtype in outs],
        in_specs=[pl.BlockSpec(memory_space=space) for space in spaces],
        out_specs=[pl.BlockSpec(memory_space=pltpu.VMEM)] * len(outs),
        scratch_shapes=scratch,
        compiler_params=pltpu.CompilerParams(vmem_limit_bytes=limit),
    )(*operands)


def on_device(embeddings, start_basis, pair_mask):
    f32, bf16 = jnp.float32, jnp.bfloat16
    wide = 2 * BLOCK
    _, parity, half = place()

    own_start = start_basis.T
    mate_start = swap_core(own_start)
    main, rest, sent, packed = call(
        send_kernel,
        [
            ((count, WIDTH), bf16)
            for count in (MAIN + 16, HALF - MAIN, HALF + 16, BLOCK + 16)
        ],
        (pair_mask, embeddings),
        scratch=[
            pltpu.SMEM((1, REACH), jnp.int32),
            pltpu.VMEM((BLOCK // PIECE, PIECE, WIDTH), f32),
            pltpu.SemaphoreType.DMA,
            pltpu.SemaphoreType.DMA((BLOCK // PIECE,)),
        ],
        far_operands=2,
    )
    far = move(main, FAR, -1)
    far_rest = move(rest, FAR, -1, 1)
    near = move(sent, NEAR, -1)
    mate = swap_core(packed)
    tiles = [((wide, HALF), bf16), ((1, wide), f32), ((1, wide), f32)]
    own_weights, sums = call(
        own_kernel, [((wide, QUARTER), bf16), ((1, wide), f32)], (packed, mate)
    )
    far_kernel = functools.partial(reach_kernel, FAR, 2)
    near_kernel = functools.partial(reach_kernel, NEAR, 1)
    far_weights, sums = call(far_kernel, tiles[:2], (packed, mate, far, far_rest, sums))
    near_weights, sums, turned = call(near_kernel, tiles, (packed, mate, near, sums))
    sums = sums + swap_core(turned)
    plane_sums = [sums, *other_planes(sums)]
    weights = (far_weights, near_weights, own_weights)
    terms = [((BASIS, HALF), f32), ((BASIS, HALF), f32), ((BASIS, QUARTER), f32)]

    def collect(far_term, near_term, own_term):
        total = move(near_term, NEAR, 1) + move(far_term, FAR, 1)
        blank = jnp.zeros_like(own_term)
        total = total + jnp.where(
            parity == 0,
            jnp.concatenate([own_term, blank], axis=1),
            jnp.concatenate([blank, own_term], axis=1),
        )
        same, across, both = other_planes(total)
        total = total + same
        other = across + both
        return jnp.where(
            half == 0,
            jnp.concatenate([total, other], axis=1),
            jnp.concatenate([other, total], axis=1),
        )

    far_term, near_term, own_term, root = call(
        first_kernel,
        terms + [((1, wide), f32)],
        (*plane_sums, own_start, mate_start, *weights),
    )
    first = collect(far_term, near_term, own_term)
    second = collect(*call(second_kernel, terms, (root, first, swap_core(first), *weights)))
    image, products = call(
        products_kernel, [((BASIS, BLOCK), f32), ((BASIS + 8, 128), f32)], (root, first, second)
    )
    products = products + swap_core(products)
    for group in ((16, 24, 8), (3, 2, 1)):
        three, two, one = [other_chip(products, bits) for bits in group]
        products = (three + two) + (one + products)
    products = products + other_chip(products, 7)
    basis, projected = call(
        finish_kernel, [((BASIS, BLOCK), f32), ((BASIS, BASIS), f32)], (products, image)
    )
    return basis.T, projected


def solution(mesh):
    grid = Mesh(mesh.devices.reshape(CHIPS, CORES, PAIRS), ALL_AXES)
    rows = P(("chip", "core"), None)
    return jax.shard_map(
        on_device, mesh=grid, in_specs=(rows, rows, rows), out_specs=(rows, P()), check_vma=False
    )
```

```python
import math

import jax
import jax.numpy as jnp
from jax import lax
from jax.experimental import pallas as pl
from jax.experimental.pallas import tpu as pltpu
from jax.sharding import Mesh
from jax.sharding import PartitionSpec as P

WIDTH = 512
BASIS = 64
BLOCK = 512
HALF = BLOCK // 2
QUARTER = BLOCK // 4
DOCS = 32768
REACH = 5
CHUNK = 256
STEP = 16
PIECE = 64
MAIN = 192
EXPONENT = -math.log(BLOCK / 4) / (2 * WIDTH) * math.log2(math.e)
UNLISTED = -1e30
CHIPS = 32
CORES = 2
PAIRS = 4
PARITIES = (0, 1, 1, 0)
HALVES = (0, 0, 1, 1)
NEAR = (1, -1)
FAR = (-2, 2)
ALL_AXES = ("chip", "core", "pairs")
NT = (((1,), (1,)), ((), ()))
EXACT = lax.Precision.HIGHEST


def move(array, reaches, sign, across=0):
    moves = []
    for chip in range(CHIPS):
        for core in range(CORES):
            for pair in range(PAIRS):
                to_pair = pair ^ across
                to_chip = (chip + sign * reaches[PARITIES[to_pair]]) % CHIPS
                source = (chip * CORES + core) * PAIRS + pair
                target = (to_chip * CORES + core) * PAIRS + to_pair
                moves.append((source, target))
    return lax.ppermute(array, ALL_AXES, moves)


def swap_core(array):
    return lax.ppermute(array, "core", [(0, 1), (1, 0)])


def other_chip(array, bits, core_bit=0):
    count = CHIPS * CORES
    return lax.ppermute(
        array, ("chip", "core"), [(i, i ^ (CORES * bits + core_bit)) for i in range(count)]
    )


def other_planes(array):
    return [
        lax.ppermute(array, "pairs", [(i, step(i)) for i in range(PAIRS)])
        for step in (lambda i: i ^ 1, lambda i: PAIRS - 1 - i, lambda i: i ^ 2)
    ]


def place():
    pair = lax.axis_index("pairs")
    parity = jnp.where((pair == 1) | (pair == 2), 1, 0)
    return lax.axis_index("core"), parity, jnp.where(pair >= 2, 1, 0)


def mask_rows(mask_ref):
    lane = lax.broadcasted_iota(jnp.int32, (16, WIDTH), 1)
    row = jnp.zeros((16, WIDTH), jnp.float32)
    for offset in range(REACH):
        row = jnp.where(lane == offset, mask_ref[0, offset].astype(jnp.float32), row)
    return row.astype(jnp.bfloat16)


def send_kernel(
    mask_ref, embeddings_ref, main_out, rest_out, sent_out, full_out,
    mask, rows, mask_arrived, rows_arrived,
):
    half = place()[2]
    mask_copy = pltpu.make_async_copy(mask_ref, mask, mask_arrived)
    mask_copy.start()
    pieces = HALF // PIECE
    copies = []
    for part in range(2 * pieces):
        which = half if part < pieces else 1 - half
        first = pl.multiple_of(which * HALF + part % pieces * PIECE, PIECE)
        source = embeddings_ref.at[pl.ds(first, PIECE), :]
        copies.append((first, pltpu.make_async_copy(source, rows.at[part], rows_arrived.at[part])))
        copies[-1][1].start()
    for part, (place_in_block, copy) in enumerate(copies):
        copy.wait()
        first = part * PIECE
        piece = rows[part].astype(jnp.bfloat16)
        full_out[pl.ds(place_in_block, PIECE), :] = piece
        if part < pieces:
            sent_out[first : first + PIECE, :] = piece
            if first < MAIN:
                main_out[first : first + PIECE, :] = piece
            else:
                rest_out[first - MAIN : first - MAIN + PIECE, :] = piece
    mask_copy.wait()
    row = mask_rows(mask)
    sent_out[HALF:, :] = row
    main_out[MAIN:, :] = row
    full_out[BLOCK:, :] = row


def column_bias(reach, own_mask, mate_mask, other_mask, core):
    lane = lax.broadcasted_iota(jnp.int32, (1, 128), 1)
    found = []
    for mask, row_core in ((own_mask, core), (mate_mask, 1 - core)):
        offset = 2 * reach + core - row_core
        ahead = jnp.where((lane == offset) & (lane < REACH), mask, 0.0)
        behind = jnp.where((lane == -offset) & (lane > 0) & (lane < REACH), other_mask, 0.0)
        flag = jnp.sum(ahead + behind, axis=1, keepdims=True)
        found.append(jnp.where(flag > 0, 0.0, UNLISTED))
    return found


def mask_row(ref):
    return ref[ref.shape[0] - 16 :, :128].astype(jnp.float32)[:1]


def norms(array):
    return EXPONENT * jnp.sum(jnp.square(array.astype(jnp.float32)), axis=1, keepdims=True)


def write_tiles(row_refs, biases, cols, out_ref):
    count = cols.shape[0]
    cols_sq = jnp.broadcast_to(norms(cols), (count, 128)).T[:1]
    for part, (row_ref, bias) in enumerate(zip(row_refs, biases)):
        shift = cols_sq + bias
        for first in range(0, BLOCK, CHUNK):
            rows = row_ref[first : first + CHUNK, :]
            inner = lax.dot_general(rows, cols, NT, preferred_element_type=jnp.float32)
            tile = jnp.exp2(inner * (-2.0 * EXPONENT) + norms(rows) + shift)
            start = part * BLOCK + first
            out_ref[start : start + CHUNK, :] = tile.astype(jnp.bfloat16)
    ones = jnp.ones((8, count), jnp.bfloat16)
    return lax.dot_general(ones, out_ref[...], NT, preferred_element_type=jnp.float32)[:1]


def own_kernel(own_ref, mate_ref, own_out, sum_out):
    core, parity, half = place()
    masks = mask_row(own_ref), mask_row(mate_ref)
    bias = column_bias(0, *masks, masks[0], core)
    start = pl.multiple_of((2 * half + parity) * QUARTER, QUARTER)
    cols = own_ref[pl.ds(start, QUARTER), :]
    sum_out[...] = write_tiles((own_ref, mate_ref), bias, cols, own_out)


def reach_kernel(
    own_ref, mate_ref, main_ref, rest_ref, near_ref, sum_ref, far_out, near_out, sum_out, turned_out
):
    core, parity, _ = place()
    masks = mask_row(own_ref), mask_row(mate_ref)
    rows = (own_ref, mate_ref)
    reach = jnp.where(parity == 0, NEAR[0], NEAR[1])
    bias = column_bias(reach, *masks, mask_row(near_ref), core)
    total = sum_ref[...] + write_tiles(rows, bias, near_ref[:HALF, :], near_out)
    reach = jnp.where(parity == 0, FAR[0], FAR[1])
    bias = column_bias(reach, *masks, mask_row(main_ref), core)
    cols = jnp.concatenate([main_ref[:MAIN, :], rest_ref[...]])
    total = total + write_tiles(rows, bias, cols, far_out)
    sum_out[...] = total
    turned_out[...] = jnp.concatenate([total[:, BLOCK:], total[:, :BLOCK]], axis=1)


def multiply(vectors, far_ref, near_ref, own_ref, far_out, near_out, own_out):
    for weights_ref, out_ref in ((far_ref, far_out), (near_ref, near_out), (own_ref, own_out)):
        found = jnp.dot(vectors, weights_ref[...], preferred_element_type=jnp.float32)
        if found.shape[0] > BASIS:
            found = found[:BASIS] + found[BASIS:]
        out_ref[...] = found


def first_kernel(
    sum_ref, same_ref, across_ref, both_ref, own_start, mate_start, far, near, own,
    far_out, near_out, own_out, root_out,
):
    degree = (sum_ref[...] + same_ref[...]) + (across_ref[...] + both_ref[...])
    root = lax.rsqrt(degree)
    root_out[...] = root
    scaled = jnp.concatenate(
        [own_start[...] * root[:, :BLOCK], mate_start[...] * root[:, BLOCK:]], axis=1
    )
    multiply(scaled.astype(jnp.bfloat16), far, near, own, far_out, near_out, own_out)


def second_kernel(root_ref, own_ref, mate_ref, far, near, own, far_out, near_out, own_out):
    root = root_ref[...]
    scaled = jnp.concatenate([own_ref[...], mate_ref[...]], axis=1) * root * root
    high = scaled.astype(jnp.bfloat16)
    low = (scaled - high.astype(jnp.float32)).astype(jnp.bfloat16)
    multiply(jnp.concatenate([high, low]), far, near, own, far_out, near_out, own_out)


def products_kernel(root_ref, first_ref, second_ref, image_out, products_out):
    root = root_ref[:, :BLOCK]
    image = second_ref[...] * root
    image_out[...] = image
    both = jnp.concatenate([first_ref[...] * root, image])
    found = lax.dot_general(both, both, NT, precision=EXACT, preferred_element_type=jnp.float32)
    row = lax.broadcasted_iota(jnp.int32, (BASIS, BASIS), 0)
    lane = lax.broadcasted_iota(jnp.int32, (BASIS, BASIS), 1)
    gram = found[BASIS:, BASIS:]
    square = jnp.where(row >= lane, found[:BASIS, :BASIS], gram)
    diagonal = jnp.sum(jnp.where(row == lane, gram, 0.0), axis=0, keepdims=True)
    products_out[:BASIS, :] = jnp.concatenate([square, found[:BASIS, BASIS:]], axis=1)
    products_out[BASIS:, :] = jnp.broadcast_to(
        jnp.concatenate([diagonal, diagonal], axis=1), (8, 2 * BASIS)
    )


def finish_kernel(products_ref, image_ref, basis_ref, projected_ref):
    square = products_ref[:BASIS, :BASIS]
    turned = square.T
    row = lax.broadcasted_iota(jnp.int32, (BASIS, BASIS), 0)
    lane = lax.broadcasted_iota(jnp.int32, (BASIS, BASIS), 1)
    first = jnp.where(row >= lane, square, turned)
    second = jnp.where(row > lane, turned, square)
    second = jnp.where(row == lane, products_ref[BASIS : BASIS + 1, :BASIS], second)
    work = jnp.concatenate([first, second], axis=1) * (1.0 / DOCS)
    row = lax.broadcasted_iota(jnp.int32, (BASIS, 128), 0)
    lane = lax.broadcasted_iota(jnp.int32, (BASIS, 128), 1)
    left = lane < BASIS
    for start in range(0, BASIS, STEP):
        columns = [
            jnp.take_along_axis(work, jnp.where(left, j, BASIS + j), axis=1)
            for j in range(start, start + STEP)
        ]
        rows = [work[j : j + 1, :] for j in range(start, start + STEP)]
        for k in range(STEP):
            j = start + k
            factor = jnp.where(row > j, columns[k] * (1.0 / columns[k][j : j + 1, :]), 0.0)
            pivot_row = rows[k] + jnp.where(lane[:1] % BASIS == j, 1.0, 0.0)
            for later in range(k + 1, STEP):
                columns[later] = columns[later] - factor * columns[later][j : j + 1, :]
                rows[later] = rows[later] - factor[start + later : start + later + 1, :] * pivot_row
            work = work - factor * pivot_row
    diagonal = lane % BASIS == row
    pivots = jnp.where(diagonal, work, 0.0)
    scale = jnp.where(
        left,
        jnp.sum(pivots[:, :BASIS], axis=1, keepdims=True),
        jnp.sum(pivots[:, BASIS:], axis=1, keepdims=True),
    )
    inverse = jnp.where(diagonal, 1.0, jnp.where(lane % BASIS < row, work, 0.0)) * lax.rsqrt(scale)
    cross = products_ref[:BASIS, BASIS:]
    first = inverse[:, :BASIS]
    half = jnp.dot(
        first, cross * (1.0 / DOCS), precision=EXACT, preferred_element_type=jnp.float32
    )
    projected_ref[...] = lax.dot_general(
        half, first, NT, precision=EXACT, preferred_element_type=jnp.float32
    )
    basis_ref[...] = jnp.dot(
        inverse[:, BASIS:], image_ref[...], precision=EXACT, preferred_element_type=jnp.float32
    )


def call(kernel, outs, operands, scratch=(), far_operands=0):
    spaces = [pl.ANY] * far_operands + [pltpu.VMEM] * (len(operands) - far_operands)
    limit = None if far_operands else 32 * 2**20
    return pl.pallas_call(
        kernel,
        out_shape=[jax.ShapeDtypeStruct(shape, dtype) for shape, dtype in outs],
        in_specs=[pl.BlockSpec(memory_space=space) for space in spaces],
        out_specs=[pl.BlockSpec(memory_space=pltpu.VMEM)] * len(outs),
        scratch_shapes=scratch,
        compiler_params=pltpu.CompilerParams(vmem_limit_bytes=limit),
    )(*operands)


def on_device(embeddings, start_basis, pair_mask):
    f32, bf16 = jnp.float32, jnp.bfloat16
    wide = 2 * BLOCK
    _, parity, half = place()

    own_start = start_basis.T
    mate_start = swap_core(own_start)
    main, rest, sent, packed = call(
        send_kernel,
        [
            ((count, WIDTH), bf16)
            for count in (MAIN + 16, HALF - MAIN, HALF + 16, BLOCK + 16)
        ],
        (pair_mask, embeddings),
        scratch=[
            pltpu.SMEM((1, REACH), jnp.int32),
            pltpu.VMEM((BLOCK // PIECE, PIECE, WIDTH), f32),
            pltpu.SemaphoreType.DMA,
            pltpu.SemaphoreType.DMA((BLOCK // PIECE,)),
        ],
        far_operands=2,
    )
    far = move(main, FAR, -1)
    far_rest = move(rest, FAR, -1, 1)
    near = move(sent, NEAR, -1)
    mate = swap_core(packed)
    own_weights, sums = call(
        own_kernel, [((wide, QUARTER), bf16), ((1, wide), f32)], (packed, mate)
    )
    tiles = ((wide, HALF), bf16)
    far_weights, near_weights, sums, turned = call(
        reach_kernel,
        [tiles, tiles, ((1, wide), f32), ((1, wide), f32)],
        (packed, mate, far, far_rest, near, sums),
    )
    sums = sums + swap_core(turned)
    plane_sums = [sums, *other_planes(sums)]
    weights = (far_weights, near_weights, own_weights)
    terms = [((BASIS, HALF), f32), ((BASIS, HALF), f32), ((BASIS, QUARTER), f32)]

    def collect(far_term, near_term, own_term):
        total = move(near_term, NEAR, 1) + move(far_term, FAR, 1)
        blank = jnp.zeros_like(own_term)
        total = total + jnp.where(
            parity == 0,
            jnp.concatenate([own_term, blank], axis=1),
            jnp.concatenate([blank, own_term], axis=1),
        )
        same, across, both = other_planes(total)
        total = total + same
        other = across + both
        return jnp.where(
            half == 0,
            jnp.concatenate([total, other], axis=1),
            jnp.concatenate([other, total], axis=1),
        )

    far_term, near_term, own_term, root = call(
        first_kernel,
        terms + [((1, wide), f32)],
        (*plane_sums, own_start, mate_start, *weights),
    )
    first = collect(far_term, near_term, own_term)
    second = collect(*call(second_kernel, terms, (root, first, swap_core(first), *weights)))
    image, products = call(
        products_kernel, [((BASIS, BLOCK), f32), ((BASIS + 8, 128), f32)], (root, first, second)
    )
    products = products + swap_core(products)
    for group in ((16, 24, 8), (3, 2, 1)):
        three, two, one = [other_chip(products, bits) for bits in group]
        products = (three + two) + (one + products)
    products = products + other_chip(products, 7)
    basis, projected = call(
        finish_kernel, [((BASIS, BLOCK), f32), ((BASIS, BASIS), f32)], (products, image)
    )
    return basis.T, projected


def solution(mesh):
    grid = Mesh(mesh.devices.reshape(CHIPS, CORES, PAIRS), ALL_AXES)
    rows = P(("chip", "core"), None)
    return jax.shard_map(
        on_device, mesh=grid, in_specs=(rows, rows, rows), out_specs=(rows, P()), check_vma=False
    )
```
